512 devices in a mesh: dp: 32 (over y_lo, z, core), row: 4 (over y_hi), col: 4 (over x).
Axes of the slice: x: 4, y: 8 (y_hi: 4, y_lo: 2; y = y_hi * 2 + y_lo), z: 8, core: 2. Of those that a mesh axis runs over, the one named last changes fastest.
Arguments:
- heads_out: bfloat16 [8192, 6144], P(('dp', 'col'), 'row'), may hold values from -6 to 6
- residual: bfloat16 [8192, 6144], P('dp', 'col'), may hold values from -6 to 6
- master: float32 [6144, 6144], P(('row', 'dp'), 'col'), may hold values from -6 to 6
- moment_one: float32 [6144, 6144], P(('row', 'dp'), 'col'), may hold values from -4 to 4
- moment_two: float32 [6144, 6144], P(('row', 'dp'), 'col'), may hold values from 0.05 to 2
- out_grad: bfloat16 [8192, 6144], P('dp', 'col'), may hold values from -6 to 6
Outputs:
- stream_out: bfloat16 [8192, 6144], P('dp', 'col')
- heads_grad: bfloat16 [8192, 6144], P(('dp', 'col'), 'row')
- weight_grad: float32 [6144, 6144], P(('row', 'dp'), 'col')
- new_master: float32 [6144, 6144], P(('row', 'dp'), 'col')
- new_moment_one: float32 [6144, 6144], P(('row', 'dp'), 'col')
- new_moment_two: float32 [6144, 6144], P(('row', 'dp'), 'col')
The draws below stay inside these ranges and needn't reach their ends.
All inputs are finite; a program needn't handle non-finite values.
Results may differ from the reference program's by a relative error of at most 0.009.
Values may be sent and summed in bfloat16 or wider, within the bound.
A program may use at most 64 MiB of HBM per device.

```python
import math
import jax
import jax.numpy as jnp
from jax import lax

DMODEL = 6144
TOK = 256
KDIM = 6144
TOKENS = 8192
N_DP = 32
N_ROW = 4
N_COL = 4


def block_levels(stream_key, shape, shards, smallest, top_value):
    level = 1.0
    for dim, blocks in shards:
        draws = jax.random.uniform(jax.random.fold_in(jax.random.fold_in(stream_key, 6), dim), (blocks,), jnp.float32, smallest / len(shards), top_value / len(shards))
        level = level * jnp.repeat(jnp.exp(draws), shape[dim] // blocks).reshape((-1,) + (1,) * (len(shape) - 1 - dim))
    return level


def bell_draw(own_key, shape, deviation, bound, split=(), kind=jnp.bfloat16):
    result = deviation * jax.random.normal(own_key, shape, jnp.float32)
    if split:
        result = result * block_levels(own_key, shape, split, -0.22, 0.18)
    return jnp.clip(result, -bound, bound).astype(kind)


def setup_inputs(seed: int = 0) -> dict:
    key_list = jax.random.split(jax.random.key(seed), 7)
    return {
        "heads_out": bell_draw(key_list[0], (TOKENS, KDIM), 1.0, 6.0, ((0, 128), (1, 4))),
        "residual": bell_draw(key_list[1], (TOKENS, DMODEL), 1.0, 6.0, ((0, 32), (1, 4))),
        "master": bell_draw(key_list[2], (KDIM, DMODEL), 1.0, 6.0, ((0, 128), (1, 4)), jnp.float32),
        "moment_one": bell_draw(key_list[3], (KDIM, DMODEL), 0.5, 4.0, ((0, 128), (1, 4)), jnp.float32),
        "moment_two": jnp.clip(jnp.exp(math.log(2.0) - 3.6888794 * jax.random.uniform(key_list[4], (KDIM, DMODEL), jnp.float32) ** block_levels(key_list[4], (KDIM, DMODEL), ((0, 128), (1, 4)), -0.2, 0.2)), 0.05, 2.0),
        "out_grad": bell_draw(key_list[5], (TOKENS, DMODEL), 1.0, 6.0, ((0, 32), (1, 4))),
    }


beta_one = 0.9
beta_two = 0.95
learn_rate = 0.1
weight_decay = 0.1
epsilon = 1e-08

def rounded(value):
    return lax.optimization_barrier(value.astype(jnp.bfloat16)).astype(jnp.float32)

def product(left, right):
    return jnp.dot(left, right, precision=lax.Precision.HIGHEST, preferred_element_type=jnp.float32)

def reference(heads_out, residual, master, moment_one, moment_two, out_grad):
    fan_scale = 1.0 / math.sqrt(KDIM)
    weight = master.astype(jnp.bfloat16).astype(jnp.float32)
    inputs = heads_out.astype(jnp.float32)
    cotangent = out_grad.astype(jnp.float32)
    k_block = KDIM // N_ROW
    n_block = DMODEL // N_COL
    mixed_sum = jnp.zeros((TOKENS, DMODEL), jnp.float32)
    for row_index in range(N_ROW):
        lower = row_index * k_block
        partial_sum = product(inputs[:, lower:lower + k_block], weight[lower:lower + k_block, :]) * fan_scale
        mixed_sum = mixed_sum + rounded(partial_sum)
    stream_out = (residual.astype(jnp.float32) + mixed_sum).astype(jnp.bfloat16)
    head_total = jnp.zeros((TOKENS, KDIM), jnp.float32)
    for col_index in range(N_COL):
        lower = col_index * n_block
        term = product(cotangent[:, lower:lower + n_block], weight[:, lower:lower + n_block].T) * fan_scale
        head_total = head_total + rounded(term)
    heads_grad = head_total.astype(jnp.bfloat16)
    grouped_in = inputs.reshape(N_DP, TOK, KDIM)
    grouped_grad = cotangent.reshape(N_DP, TOK, DMODEL)

    def add_group(carried, pair):
        group_in, group_grad = pair
        return (carried + rounded(product(group_in.T, group_grad) * fan_scale), None)
    weight_grad, _ = lax.scan(add_group, jnp.zeros((KDIM, DMODEL), jnp.float32), (grouped_in, grouped_grad))
    new_moment_one = beta_one * moment_one + (1.0 - beta_one) * weight_grad
    new_moment_two = beta_two * moment_two + (1.0 - beta_two) * weight_grad * weight_grad
    bias_one = 1.0 - beta_one ** 10
    bias_two = 1.0 - beta_two ** 10
    direction = new_moment_one / bias_one / (jnp.sqrt(new_moment_two / bias_two) + epsilon)
    new_master = master - learn_rate * (direction + weight_decay * master)
    return (stream_out, heads_grad, weight_grad, new_master, new_moment_one, new_moment_two)
```

```python
import math

import jax
import jax.numpy as jnp
from jax import lax
from jax.experimental import pallas as pl
from jax.experimental.pallas import tpu as pltpu
from jax.sharding import PartitionSpec as P

HEADS = 48
HEAD_DIM = 128

beta_one = 0.9
beta_two = 0.95
learn_rate = 0.1
weight_decay = 0.1
epsilon = 1e-08

MESH = pl.DeviceIdType.MESH
BF16, F32 = jnp.bfloat16, jnp.float32

NX, NY, NZ = 4, 8, 8
TOK = 256
QTOK = 64
KHALF = 768
COLS = 1536
NHALF = 768
ROWS = 48
SIDES = (1, -1)
SCALE = 1.0 / math.sqrt(HEADS * HEAD_DIM)


def reach(part, side, around):
    longer = around // 2
    return longer if (part == 0) == (side == 0) else around - 1 - longer


def kernel(
    h_ref, res_ref, master_ref, m1_ref, m2_ref, g_ref,
    stream_ref, hgrad_ref, wg_ref, nm_ref, n1_ref, n2_ref,
    hbuf, gbuf, wbuf, yp, ysend, yrecv, yout, resv,
    hp, hsend, hrecv, hfin, dwp, dwx_send, dwx_recv, dsend, drecv,
    mv, m1v, m2v, wgv, nmv, n1v, n2v,
    wz_s, wz_r, wc_s, wc_r, hx_s, hx_r, gx_s, gx_r, y_s, y_r, ya_s, ya_r,
    dh_s, dh_r, hy_s, hy_r, dx_s, dx_r, dz_s, dz_r, loc,
):
    dp, yh, x = lax.axis_index("dp"), lax.axis_index("row"), lax.axis_index("col")
    c = lax.rem(dp, 2)
    z = lax.rem(lax.div(dp, 2), NZ)
    yl = lax.div(dp, 2 * NZ)
    y = 2 * yh + yl

    def wrap(v, n):
        return lax.rem(v + n, n)

    def device(dx=0, dy=0, dz=0, flip=False):
        yy = wrap(y + dy, NY)
        core = 1 - c if flip else c
        return ((lax.rem(yy, 2) * NZ + wrap(z + dz, NZ)) * 2 + core, lax.div(yy, 2), wrap(x + dx, NX))

    to_partner = 1 - 2 * yl
    zdev = [device(dz=s) for s in SIDES]
    xdev = [device(dx=s) for s in SIDES]
    ydev = [device(dy=s) for s in SIDES]
    y2dev = [device(dy=2 * s) for s in SIDES]
    cdev = device(flip=True)
    pdev = device(dy=to_partner)
    hidev = device(dy=-to_partner)

    sent = []

    def remote(src, dst, ssem, rsem, dev):
        return pltpu.make_async_remote_copy(
            src_ref=src, dst_ref=dst, send_sem=ssem, recv_sem=rsem, device_id=dev, device_id_type=MESH)

    def send(src, dst, ssem, rsem, dev):
        copy = remote(src, dst, ssem, rsem, dev)
        copy.start()
        sent.append(copy)

    def arrived(dst, ssem, rsem, dev):
        remote(dst, dst, ssem, rsem, dev).wait_recv()

    def own_cols(v):
        return pl.ds(pl.multiple_of(v * KHALF, KHALF), KHALF)

    load_master = pltpu.make_async_copy(master_ref, mv, loc.at[0])
    load_master.start()
    load_h = pltpu.make_async_copy(h_ref.at[:, own_cols(yl)], hbuf.at[yl * NX + x], loc.at[1])
    load_h.start()
    load_g = pltpu.make_async_copy(g_ref, gbuf.at[pl.ds(pl.multiple_of(yl * TOK, TOK), TOK)], loc.at[2])
    load_g.start()
    load_res = pltpu.make_async_copy(
        res_ref.at[pl.ds(pl.multiple_of(yh * QTOK, QTOK), QTOK)], resv, loc.at[3])
    load_res.start()
    load_m1 = pltpu.make_async_copy(m1_ref, m1v, loc.at[4])
    load_m1.start()
    load_m2 = pltpu.make_async_copy(m2_ref, m2v, loc.at[5])
    load_m2.start()

    barrier = pltpu.get_barrier_semaphore()
    around = zdev + xdev + ydev + y2dev + [cdev]
    for dev in around:
        pl.semaphore_signal(barrier, inc=1, device_id=dev, device_id_type=MESH)
    load_master.wait()
    own = z * 2 + c
    for nh in range(2):
        wbuf[nh, own] = mv[:, nh * NHALF:(nh + 1) * NHALF].astype(BF16)
    pl.semaphore_wait(barrier, len(around))

    def wz_send(nh, side, s):
        slot = wbuf.at[nh, wrap(z - SIDES[side] * s, NZ) * 2 + c]
        send(slot, slot, wz_s.at[nh, side, s], wz_r.at[nh, side, s], zdev[side])

    def wc_send(nh, k, zz):
        slot = wbuf.at[nh, zz * 2 + c]
        send(slot, slot, wc_s.at[nh, k], wc_r.at[nh, k], cdev)

    def wz_step(nh, s):
        for side in range(2):
            if s <= reach(nh, side, NZ):
                zz = wrap(z - SIDES[side] * s, NZ)
                arrived(wbuf.at[nh, zz * 2 + c], wz_s.at[nh, side, s - 1], wz_r.at[nh, side, s - 1], zdev[side])
                if s < reach(nh, side, NZ):
                    wz_send(nh, side, s)
                wc_send(nh, s if side == 0 else reach(nh, 0, NZ) + s, zz)

    def wc_wait(nh):
        for k in range(NZ):
            up = reach(nh, 0, NZ)
            zz = z if k == 0 else wrap(z - k, NZ) if k <= up else wrap(z + (k - up), NZ)
            arrived(wbuf.at[nh, zz * 2 + 1 - c], wc_s.at[nh, k], wc_r.at[nh, k], cdev)

    other = 1 - yl

    def hx_send(src, slot, k, dev):
        send(src, hbuf.at[slot], hx_s.at[k], hx_r.at[k], dev)

    def h_arrived(slot, k):
        arrived(hbuf.at[slot], hx_s.at[k], hx_r.at[k], pdev)

    for side in range(2):
        wz_send(0, side, 0)
    hx_send(h_ref.at[:, own_cols(other)], yl * NX + x, 0, pdev)
    for side in range(2):
        hx_send(h_ref.at[:, own_cols(yl)], yl * NX + x, 1 + side, xdev[side])
    half = TOK // 2
    g_first = pl.ds(pl.multiple_of(other * half, half), half)
    g_there = pl.ds(pl.multiple_of(yl * TOK + other * half, half), half)
    send(g_ref.at[g_first], gbuf.at[g_there], gx_s.at[0], gx_r.at[0], hidev)
    wc_send(0, 0, z)
    for side in range(2):
        wz_send(1, side, 0)
    wc_send(1, 0, z)

    h_arrived(other * NX + x, 0)
    for side in range(2):
        hx_send(hbuf.at[other * NX + x], other * NX + x, 3 + side, xdev[side])
    g_last = pl.ds(pl.multiple_of(yl * half, half), half)
    g_goal = pl.ds(pl.multiple_of(yl * TOK + yl * half, half), half)
    send(g_ref.at[g_last], gbuf.at[g_goal], gx_s.at[1], gx_r.at[1], pdev)

    wz_step(0, 1)
    for side in range(2):
        h_arrived(yl * NX + wrap(x - SIDES[side], NX), 1 + side)
    for side in range(2):
        h_arrived(other * NX + wrap(x - SIDES[side], NX), 3 + side)
    for g in range(2):
        slot = g * NX + wrap(x - SIDES[g], NX)
        hx_send(hbuf.at[slot], slot, 5 + g, xdev[g])
    wz_step(0, 2)
    wz_step(1, 1)
    wz_step(0, 3)
    wz_step(1, 2)
    wz_step(0, 4)
    for g in range(2):
        h_arrived(g * NX + wrap(x + 2, NX), 5 + g)
    load_h.wait()
    wc_wait(0)

    def y_slot(v):
        yy = wrap(v, NY)
        return lax.rem(yy, 2) * 4 + lax.div(yy, 2)

    def y_dot(nh):
        w = wbuf[nh].reshape(KHALF, NHALF)
        h = hbuf[...].reshape(2 * TOK, KHALF)
        for t in range(NHALF // 256):
            part = jnp.dot(h, w[:, t * 256:(t + 1) * 256], preferred_element_type=F32) * SCALE
            yp[nh, :, :, t * 256:(t + 1) * 256] = part.reshape(8, QTOK, 256)

    def y_step(nh, s):
        for side in range(2):
            hops = reach(nh, side, NY)
            if s < hops:
                value = yp[nh, y_slot(y + SIDES[side] * (hops - s))]
                if s:
                    arrived(yrecv.at[nh, side, s - 1], y_s.at[nh, side, s - 1], y_r.at[nh, side, s - 1], ydev[side])
                    value = value + yrecv[nh, side, s - 1].astype(F32)
                ysend[nh, side, s] = value.astype(BF16)
                send(ysend.at[nh, side, s], yrecv.at[nh, side, s], y_s.at[nh, side, s], y_r.at[nh, side, s], ydev[side])

    def stream_place(nh, q):
        return stream_ref.at[pl.ds(pl.multiple_of(q * QTOK, QTOK), QTOK), pl.ds(nh * NHALF, NHALF)]

    stores = []

    def store(src, dst, sem):
        copy = pltpu.make_async_copy(src, dst, sem)
        copy.start()
        stores.append(copy)

    def y_final(nh):
        value = yp[nh, y_slot(y)] + resv[:, nh * NHALF:(nh + 1) * NHALF].astype(F32)
        for side in range(2):
            last = reach(nh, side, NY) - 1
            arrived(yrecv.at[nh, side, last], y_s.at[nh, side, last], y_r.at[nh, side, last], ydev[side])
            value = value + yrecv[nh, side, last].astype(F32)
        yout[nh, yh] = value.astype(BF16)
        for side in range(2):
            send(yout.at[nh, yh], yout.at[nh, yh], ya_s.at[nh, side], ya_r.at[nh, side], y2dev[side])
        store(yout.at[nh, yh], stream_place(nh, yh), loc.at[6 + nh * 4])

    def ya_arrived(nh, k, q):
        arrived(yout.at[nh, q], ya_s.at[nh, k], ya_r.at[nh, k], y2dev[0])

    def y_spread(nh):
        order = (0, 1) if nh == 0 else (1, 0)
        for side in order:
            q = wrap(yh - SIDES[side], 4)
            ya_arrived(nh, side, q)
            if side == nh:
                send(yout.at[nh, q], yout.at[nh, q], ya_s.at[nh, 2], ya_r.at[nh, 2], y2dev[side])
            store(yout.at[nh, q], stream_place(nh, q), loc.at[7 + nh * 4 + side])

    def y_end(nh):
        q = wrap(yh + 2, 4)
        ya_arrived(nh, 2, q)
        store(yout.at[nh, q], stream_place(nh, q), loc.at[9 + nh * 4])

    def h_dot():
        for t in range(2):
            rows = pl.ds(t * 256, 256)
            total = None
            for nh in range(2):
                w = wbuf[nh].reshape(KHALF, NHALF)
                part = lax.dot_general(
                    gbuf[rows, nh * NHALF:(nh + 1) * NHALF], w, (((1,), (1,)), ((), ())),
                    preferred_element_type=F32)
                total = part if total is None else total + part
            hp[t * 4:(t + 1) * 4] = (total * SCALE).reshape(4, QTOK, KHALF)

    def h_step(s):
        for g in range(2):
            for side in range(2):
                hops = reach(g, side, NX)
                if s < hops:
                    value = hp[g * NX + wrap(x + SIDES[side] * (hops - s), NX)]
                    if s:
                        arrived(hrecv.at[g, side, s - 1], dh_s.at[g, side, s - 1], dh_r.at[g, side, s - 1], xdev[side])
                        value = value + hrecv[g, side, s - 1].astype(F32)
                    hsend[g, side, s] = value.astype(BF16)
                    send(hsend.at[g, side, s], hrecv.at[g, side, s], dh_s.at[g, side, s], dh_r.at[g, side, s], xdev[side])

    def h_final():
        for g in range(2):
            value = hp[g * NX + x]
            for side in range(2):
                last = reach(g, side, NX) - 1
                arrived(hrecv.at[g, side, last], dh_s.at[g, side, last], dh_r.at[g, side, last], xdev[side])
                value = value + hrecv[g, side, last].astype(F32)
            hfin[g] = value.astype(BF16)
        send(hfin.at[other], hgrad_ref.at[:, own_cols(yl)], hy_s, hy_r, pdev)
        store(hfin.at[yl], hgrad_ref.at[:, own_cols(yl)], loc.at[14])

    def d_dot():
        h = hbuf[...].reshape(2 * TOK, KHALF)
        for t in range(COLS // 256):
            part = lax.dot_general(
                h, gbuf[:, t * 256:(t + 1) * 256], (((0,), (0,)), ((), ())), preferred_element_type=F32)
            dwp[:, :, t * 256:(t + 1) * 256] = (part * SCALE).reshape(16, ROWS, 256)

    def d_cross():
        for zz in range(NZ):
            dwx_send[zz] = dwp[zz * 2 + 1 - c].astype(BF16)
        send(dwx_send, dwx_recv, dx_s, dx_r, cdev)

    def d_piece(nh, zz):
        cols = slice(nh * NHALF, (nh + 1) * NHALF)
        return dwp[zz * 2 + c, :, cols] + dwx_recv[zz, :, cols].astype(F32)

    def d_step(nh, s):
        for side in range(2):
            hops = reach(nh, side, NZ)
            if s < hops:
                value = d_piece(nh, wrap(z + SIDES[side] * (hops - s), NZ))
                if s:
                    arrived(drecv.at[nh, side, s - 1], dz_s.at[nh, side, s - 1], dz_r.at[nh, side, s - 1], zdev[side])
                    value = value + drecv[nh, side, s - 1].astype(F32)
                dsend[nh, side, s] = value.astype(BF16)
                send(dsend.at[nh, side, s], drecv.at[nh, side, s], dz_s.at[nh, side, s], dz_r.at[nh, side, s], zdev[side])

    def d_final(nh):
        value = d_piece(nh, z)
        for side in range(2):
            last = reach(nh, side, NZ) - 1
            arrived(drecv.at[nh, side, last], dz_s.at[nh, side, last], dz_r.at[nh, side, last], zdev[side])
            value = value + drecv[nh, side, last].astype(F32)
        wgv[:, nh * NHALF:(nh + 1) * NHALF] = value

    def adam():
        grad = wgv[...]
        master = mv[...]
        new_one = beta_one * m1v[...] + (1.0 - beta_one) * grad
        new_two = beta_two * m2v[...] + (1.0 - beta_two) * grad * grad
        bias_one = 1.0 - beta_one**10
        bias_two = 1.0 - beta_two**10
        direction = new_one / bias_one / (jnp.sqrt(new_two / bias_two) + epsilon)
        n1v[...] = new_one
        n2v[...] = new_two
        nmv[...] = master - learn_rate * (direction + weight_decay * master)
        store(wgv, wg_ref, loc.at[15])
        store(nmv, nm_ref, loc.at[16])
        store(n1v, n1_ref, loc.at[17])
        store(n2v, n2_ref, loc.at[18])

    y_dot(0)
    y_step(0, 0)
    wz_step(1, 3)
    wz_step(1, 4)
    load_g.wait()
    arrived(gbuf.at[g_there], gx_s.at[0], gx_r.at[0], hidev)
    arrived(gbuf.at[g_goal], gx_s.at[1], gx_r.at[1], pdev)
    d_dot()
    d_cross()
    y_step(0, 1)
    wc_wait(1)
    y_dot(1)
    y_step(1, 0)
    y_step(0, 2)
    h_dot()
    h_step(0)
    y_step(1, 1)
    arrived(dwx_recv, dx_s, dx_r, cdev)
    for nh in range(2):
        d_step(nh, 0)
    y_step(0, 3)
    h_step(1)
    y_step(1, 2)
    for nh in range(2):
        d_step(nh, 1)
    load_res.wait()
    y_final(0)
    h_final()
    y_step(1, 3)
    for nh in range(2):
        d_step(nh, 2)
    y_final(1)
    y_spread(0)
    for nh in range(2):
        d_step(nh, 3)
    load_m1.wait()
    load_m2.wait()
    y_spread(1)
    for nh in range(2):
        d_final(nh)
    adam()
    y_end(0)
    arrived(hgrad_ref.at[:, own_cols(other)], hy_s, hy_r, pdev)
    y_end(1)
    for copy in stores:
        copy.wait()
    for copy in sent:
        copy.wait_send()


def shards(heads_out, residual, master, moment_one, moment_two, out_grad):
    any_spec = pl.BlockSpec(memory_space=pl.ANY)
    dma = pltpu.SemaphoreType.DMA
    vmem = pltpu.VMEM
    weights = jax.ShapeDtypeStruct((ROWS, COLS), F32)
    outs = pl.pallas_call(
        kernel,
        out_shape=(
            jax.ShapeDtypeStruct((TOK, COLS), BF16),
            jax.ShapeDtypeStruct((QTOK, COLS), BF16),
            weights, weights, weights, weights,
        ),
        in_specs=[any_spec] * 6,
        out_specs=[any_spec] * 6,
        scratch_shapes=[
            vmem((8, QTOK, KHALF), BF16),
            vmem((2 * TOK, COLS), BF16),
            vmem((2, 16, ROWS, NHALF), BF16),
            vmem((2, 8, QTOK, NHALF), F32),
            vmem((2, 2, 4, QTOK, NHALF), BF16),
            vmem((2, 2, 4, QTOK, NHALF), BF16),
            vmem((2, 4, QTOK, NHALF), BF16),
            vmem((QTOK, COLS), BF16),
            vmem((8, QTOK, KHALF), F32),
            vmem((2, 2, 2, QTOK, KHALF), BF16),
            vmem((2, 2, 2, QTOK, KHALF), BF16),
            vmem((2, QTOK, KHALF), BF16),
            vmem((16, ROWS, COLS), F32),
            vmem((8, ROWS, COLS), BF16),
            vmem((8, ROWS, COLS), BF16),
            vmem((2, 2, 4, ROWS, NHALF), BF16),
            vmem((2, 2, 4, ROWS, NHALF), BF16),
            vmem((ROWS, COLS), F32),
            vmem((ROWS, COLS), F32),
            vmem((ROWS, COLS), F32),
            vmem((ROWS, COLS), F32),
            vmem((ROWS, COLS), F32),
            vmem((ROWS, COLS), F32),
            vmem((ROWS, COLS), F32),
            dma((2, 2, 4)), dma((2, 2, 4)), dma((2, 8)), dma((2, 8)),
            dma((7,)), dma((7,)), dma((2,)), dma((2,)),
            dma((2, 2, 4)), dma((2, 2, 4)), dma((2, 3)), dma((2, 3)),
            dma((2, 2, 2)), dma((2, 2, 2)), dma, dma, dma, dma,
            dma((2, 2, 4)), dma((2, 2, 4)), dma((19,)),
        ],
        compiler_params=pltpu.CompilerParams(
            collective_id=0, has_side_effects=True, vmem_limit_bytes=48 << 20),
        cost_estimate=pl.CostEstimate(
            flops=6 * TOK * COLS * COLS, bytes_accessed=5 << 20, transcendentals=ROWS * COLS),
    )(heads_out, residual, master, moment_one, moment_two, out_grad)
    return tuple(outs)


def solution(mesh):
    return jax.shard_map(
        shards,
        mesh=mesh,
        in_specs=(
            P(("dp", "col"), "row"),
            P("dp", "col"),
            P(("row", "dp"), "col"),
            P(("row", "dp"), "col"),
            P(("row", "dp"), "col"),
            P("dp", "col"),
        ),
        out_specs=(
            P("dp", "col"),
            P(("dp", "col"), "row"),
            P(("row", "dp"), "col"),
            P(("row", "dp"), "col"),
            P(("row", "dp"), "col"),
            P(("row", "dp"), "col"),
        ),
        check_vma=False,
    )
```

```python
import math

import jax
import jax.numpy as jnp
from jax import lax
from jax.experimental import pallas as pl
from jax.experimental.pallas import tpu as pltpu
from jax.sharding import PartitionSpec as P

HEADS = 48
HEAD_DIM = 128

beta_one = 0.9
beta_two = 0.95
learn_rate = 0.1
weight_decay = 0.1
epsilon = 1e-08

MESH = pl.DeviceIdType.MESH
BF16, F32 = jnp.bfloat16, jnp.float32

NX, NY, NZ = 4, 8, 8
TOK = 256
QTOK = 64
KHALF = 768
COLS = 1536
NHALF = 768
PARTS = 4
WIDE = COLS // PARTS
ROWS = 48
SIDES = (1, -1)
SCALE = 1.0 / math.sqrt(HEADS * HEAD_DIM)


def reach(part, side, around):
    longer = around // 2
    return longer if part % 2 == side else around - 1 - longer


def kernel(
    h_ref, res_ref, master_ref, m1_ref, m2_ref, g_ref,
    yout, hgrad, wgv, nmv, n1v, n2v,
    hbuf, gbuf, wbuf, yp, ysend, yrecv, resv,
    hp, hsend, hrecv, hfin, dwp, dwx_send, dwx_recv, dsend, drecv,
    mv, m1v, m2v,
    wz_s, wz_r, wc_s, wc_r, hx_s, hx_r, gx_s, gx_r, y_s, y_r, ya_s, ya_r,
    dh_s, dh_r, hy_s, hy_r, dx_s, dx_r, dz_s, dz_r, loc,
):
    dp, yh, x = lax.axis_index("dp"), lax.axis_index("row"), lax.axis_index("col")
    c = lax.rem(dp, 2)
    z = lax.rem(lax.div(dp, 2), NZ)
    yl = lax.div(dp, 2 * NZ)
    y = 2 * yh + yl

    def wrap(v, n):
        return lax.rem(v + n, n)

    def device(dx=0, dy=0, dz=0, flip=False):
        yy = wrap(y + dy, NY)
        core = 1 - c if flip else c
        return ((lax.rem(yy, 2) * NZ + wrap(z + dz, NZ)) * 2 + core, lax.div(yy, 2), wrap(x + dx, NX))

    to_partner = 1 - 2 * yl
    zdev = [device(dz=s) for s in SIDES]
    xdev = [device(dx=s) for s in SIDES]
    ydev = [device(dy=s) for s in SIDES]
    y2dev = [device(dy=2 * s) for s in SIDES]
    cdev = device(flip=True)
    pdev = device(dy=to_partner)
    hidev = device(dy=-to_partner)

    sent = []

    def remote(src, dst, ssem, rsem, dev):
        return pltpu.make_async_remote_copy(
            src_ref=src, dst_ref=dst, send_sem=ssem, recv_sem=rsem, device_id=dev, device_id_type=MESH)

    def send(src, dst, ssem, rsem, dev):
        copy = remote(src, dst, ssem, rsem, dev)
        copy.start()
        sent.append(copy)

    def arrived(dst, ssem, rsem, dev):
        remote(dst, dst, ssem, rsem, dev).wait_recv()

    def own_cols(v):
        return pl.ds(pl.multiple_of(v * KHALF, KHALF), KHALF)

    load_master = pltpu.make_async_copy(master_ref, mv, loc.at[0])
    load_master.start()
    load_h = pltpu.make_async_copy(h_ref.at[:, own_cols(yl)], hbuf.at[yl * NX + x], loc.at[1])
    load_h.start()
    load_g = pltpu.make_async_copy(g_ref, gbuf.at[pl.ds(pl.multiple_of(yl * TOK, TOK), TOK)], loc.at[2])
    load_g.start()
    load_res = pltpu.make_async_copy(
        res_ref.at[pl.ds(pl.multiple_of(yh * QTOK, QTOK), QTOK)], resv, loc.at[3])
    load_res.start()
    load_m1 = pltpu.make_async_copy(m1_ref, m1v, loc.at[4])
    load_m1.start()
    load_m2 = pltpu.make_async_copy(m2_ref, m2v, loc.at[5])
    load_m2.start()

    def wz_send(n, side, s):
        slot = wbuf.at[n, wrap(z - SIDES[side] * s, NZ) * 2 + c]
        send(slot, slot, wz_s.at[n, side, s], wz_r.at[n, side, s], zdev[side])

    def wc_send(n, k, zz):
        slot = wbuf.at[n, zz * 2 + c]
        send(slot, slot, wc_s.at[n, k], wc_r.at[n, k], cdev)

    def wz_step(n, s):
        for side in range(2):
            if s <= reach(n, side, NZ):
                zz = wrap(z - SIDES[side] * s, NZ)
                arrived(wbuf.at[n, zz * 2 + c], wz_s.at[n, side, s - 1], wz_r.at[n, side, s - 1], zdev[side])
                if s < reach(n, side, NZ):
                    wz_send(n, side, s)
                wc_send(n, s if side == 0 else reach(n, 0, NZ) + s, zz)

    def wc_wait(n):
        for k in range(NZ):
            up = reach(n, 0, NZ)
            zz = z if k == 0 else wrap(z - k, NZ) if k <= up else wrap(z + (k - up), NZ)
            arrived(wbuf.at[n, zz * 2 + 1 - c], wc_s.at[n, k], wc_r.at[n, k], cdev)

    other = 1 - yl
    half = TOK // 2
    g_first = pl.ds(pl.multiple_of(other * half, half), half)
    g_there = pl.ds(pl.multiple_of(yl * TOK + other * half, half), half)
    g_last = pl.ds(pl.multiple_of(yl * half, half), half)
    g_goal = pl.ds(pl.multiple_of(yl * TOK + yl * half, half), half)

    def hx_send(src, slot, k, dev):
        send(src, hbuf.at[slot], hx_s.at[k], hx_r.at[k], dev)

    def h_arrived(slot, k):
        arrived(hbuf.at[slot], hx_s.at[k], hx_r.at[k], pdev)

    def h_far(g, k):
        step = 1 - 2 * g
        slot = g * NX + wrap(x - step, NX)
        hx_send(hbuf.at[slot], slot, k, device(dx=step))

    def y_slot(v):
        yy = wrap(v, NY)
        return lax.rem(yy, 2) * 4 + lax.div(yy, 2)

    def y_dot(n):
        h = hbuf[...].reshape(2 * TOK, KHALF)
        part = jnp.dot(h, wbuf[n].reshape(KHALF, WIDE), preferred_element_type=F32) * SCALE
        yp[n] = part.reshape(8, QTOK, WIDE)

    def y_step(n, s):
        for side in range(2):
            hops = reach(n, side, NY)
            if s < hops:
                value = yp[n, y_slot(y + SIDES[side] * (hops - s))]
                if s:
                    arrived(yrecv.at[n, side, s - 1], y_s.at[n, side, s - 1], y_r.at[n, side, s - 1], ydev[side])
                    value = value + yrecv[n, side, s - 1].astype(F32)
                ysend[n, side, s] = value.astype(BF16)
                send(ysend.at[n, side, s], yrecv.at[n, side, s], y_s.at[n, side, s], y_r.at[n, side, s], ydev[side])

    def y_final(n):
        value = yp[n, y_slot(y)] + resv[:, n * WIDE:(n + 1) * WIDE].astype(F32)
        for side in range(2):
            last = reach(n, side, NY) - 1
            arrived(yrecv.at[n, side, last], y_s.at[n, side, last], y_r.at[n, side, last], ydev[side])
            value = value + yrecv[n, side, last].astype(F32)
        yout[n, yh] = value.astype(BF16)
        for side in range(2):
            send(yout.at[n, yh], yout.at[n, yh], ya_s.at[n, side], ya_r.at[n, side], y2dev[side])

    def ya_arrived(n, k, q):
        arrived(yout.at[n, q], ya_s.at[n, k], ya_r.at[n, k], y2dev[0])

    def y_spread(n):
        order = (0, 1) if n % 2 == 0 else (1, 0)
        for side in order:
            q = wrap(yh - SIDES[side], 4)
            ya_arrived(n, side, q)
            if side == n % 2:
                send(yout.at[n, q], yout.at[n, q], ya_s.at[n, 2], ya_r.at[n, 2], y2dev[side])

    def y_end(n):
        q = wrap(yh + 2, 4)
        ya_arrived(n, 2, q)

    def h_dot():
        for t in range(2):
            rows = pl.ds(t * 256, 256)
            total = None
            for n in range(PARTS):
                w = wbuf[n].reshape(KHALF, WIDE)
                part = lax.dot_general(
                    gbuf[rows, n * WIDE:(n + 1) * WIDE], w, (((1,), (1,)), ((), ())),
                    preferred_element_type=F32)
                total = part if total is None else total + part
            hp[t * 4:(t + 1) * 4] = (total * SCALE).reshape(4, QTOK, KHALF)

    def h_step(s):
        for g in range(2):
            for side in range(2):
                hops = reach(g, side, NX)
                if s < hops:
                    value = hp[g * NX + wrap(x + SIDES[side] * (hops - s), NX)]
                    if s:
                        arrived(hrecv.at[g, side, s - 1], dh_s.at[g, side, s - 1], dh_r.at[g, side, s - 1], xdev[side])
                        value = value + hrecv[g, side, s - 1].astype(F32)
                    hsend[g, side, s] = value.astype(BF16)
                    send(hsend.at[g, side, s], hrecv.at[g, side, s], dh_s.at[g, side, s], dh_r.at[g, side, s], xdev[side])

    def h_final():
        for g in range(2):
            value = hp[g * NX + x]
            for side in range(2):
                last = reach(g, side, NX) - 1
                arrived(hrecv.at[g, side, last], dh_s.at[g, side, last], dh_r.at[g, side, last], xdev[side])
                value = value + hrecv[g, side, last].astype(F32)
            hfin[g] = value.astype(BF16)
        send(hfin.at[other], hgrad.at[yl], hy_s, hy_r, pdev)
        hgrad[yl] = hfin[yl]

    def d_dot():
        h = hbuf[...].reshape(2 * TOK, KHALF)
        for t in range(COLS // 256):
            part = lax.dot_general(
                h, gbuf[:, t * 256:(t + 1) * 256], (((0,), (0,)), ((), ())), preferred_element_type=F32)
            dwp[:, :, t * 256:(t + 1) * 256] = (part * SCALE).reshape(16, ROWS, 256)

    def d_cross():
        for zz in range(NZ):
            dwx_send[zz] = dwp[zz * 2 + 1 - c].astype(BF16)
        send(dwx_send, dwx_recv, dx_s, dx_r, cdev)

    def d_piece(nh, zz):
        cols = slice(nh * NHALF, (nh + 1) * NHALF)
        return dwp[zz * 2 + c, :, cols] + dwx_recv[zz, :, cols].astype(F32)

    def d_step(nh, s):
        for side in range(2):
            hops = reach(nh, side, NZ)
            if s < hops:
                value = d_piece(nh, wrap(z + SIDES[side] * (hops - s), NZ))
                if s:
                    arrived(drecv.at[nh, side, s - 1], dz_s.at[nh, side, s - 1], dz_r.at[nh, side, s - 1], zdev[side])
                    value = value + drecv[nh, side, s - 1].astype(F32)
                dsend[nh, side, s] = value.astype(BF16)
                send(dsend.at[nh, side, s], drecv.at[nh, side, s], dz_s.at[nh, side, s], dz_r.at[nh, side, s], zdev[side])

    def d_final(nh):
        value = d_piece(nh, z)
        for side in range(2):
            last = reach(nh, side, NZ) - 1
            arrived(drecv.at[nh, side, last], dz_s.at[nh, side, last], dz_r.at[nh, side, last], zdev[side])
            value = value + drecv[nh, side, last].astype(F32)
        wgv[:, nh * NHALF:(nh + 1) * NHALF] = value

    def adam():
        grad = wgv[...]
        master = mv[...]
        new_one = beta_one * m1v[...] + (1.0 - beta_one) * grad
        new_two = beta_two * m2v[...] + (1.0 - beta_two) * grad * grad
        bias_one = 1.0 - beta_one**10
        bias_two = 1.0 - beta_two**10
        direction = new_one / bias_one / (jnp.sqrt(new_two / bias_two) + epsilon)
        n1v[...] = new_one
        n2v[...] = new_two
        nmv[...] = master - learn_rate * (direction + weight_decay * master)

    barrier = pltpu.get_barrier_semaphore()
    around = zdev + xdev + ydev + y2dev + [cdev]
    for dev in around:
        pl.semaphore_signal(barrier, inc=1, device_id=dev, device_id_type=MESH)
    load_master.wait()
    own = z * 2 + c
    for n in range(PARTS):
        wbuf[n, own] = mv[:, n * WIDE:(n + 1) * WIDE].astype(BF16)
    pl.semaphore_wait(barrier, len(around))

    for side in range(2):
        wz_send(0, side, 0)
    hx_send(h_ref.at[:, own_cols(other)], yl * NX + x, 0, pdev)
    for side in range(2):
        hx_send(h_ref.at[:, own_cols(yl)], yl * NX + x, 1 + side, xdev[side])
    wc_send(0, 0, z)
    for side in range(2):
        wz_send(1, side, 0)
    send(g_ref.at[g_first], gbuf.at[g_there], gx_s.at[0], gx_r.at[0], hidev)
    wc_send(1, 0, z)
    for n in range(2, PARTS):
        for side in range(2):
            wz_send(n, side, 0)
        wc_send(n, 0, z)

    wz_step(0, 1)
    wz_step(1, 1)
    h_arrived(other * NX + x, 0)
    for side in range(2):
        hx_send(hbuf.at[other * NX + x], other * NX + x, 3 + side, xdev[side])
    send(g_ref.at[g_last], gbuf.at[g_goal], gx_s.at[1], gx_r.at[1], pdev)
    wz_step(2, 1)
    wz_step(3, 1)
    for side in range(2):
        h_arrived(yl * NX + wrap(x - SIDES[side], NX), 1 + side)
    h_far(yl, 5)
    wz_step(0, 2)
    wz_step(1, 2)
    wz_step(2, 2)
    for side in range(2):
        h_arrived(other * NX + wrap(x - SIDES[side], NX), 3 + side)
    h_far(other, 6)
    wz_step(3, 2)
    for n in range(PARTS):
        wz_step(n, 3)
    wz_step(0, 4)
    load_h.wait()
    h_arrived(yl * NX + wrap(x + 2, NX), 5)
    h_arrived(other * NX + wrap(x + 2, NX), 6)
    wc_wait(0)
    y_dot(0)
    y_step(0, 0)
    wz_step(1, 4)
    wz_step(2, 4)
    wz_step(3, 4)
    wc_wait(1)
    y_dot(1)
    y_step(1, 0)
    wc_wait(2)
    y_dot(2)
    y_step(2, 0)
    y_step(0, 1)
    wc_wait(3)
    y_dot(3)
    y_step(3, 0)
    load_g.wait()
    arrived(gbuf.at[g_there], gx_s.at[0], gx_r.at[0], hidev)
    arrived(gbuf.at[g_goal], gx_s.at[1], gx_r.at[1], pdev)
    y_step(1, 1)
    d_dot()
    d_cross()
    y_step(2, 1)
    y_step(0, 2)
    y_step(3, 1)
    h_dot()
    h_step(0)
    y_step(1, 2)
    y_step(2, 2)
    arrived(dwx_recv, dx_s, dx_r, cdev)
    for nh in range(2):
        d_step(nh, 0)
    y_step(0, 3)
    y_step(3, 2)
    y_step(1, 3)
    h_step(1)
    y_step(2, 3)
    load_res.wait()
    y_final(0)
    for nh in range(2):
        d_step(nh, 1)
    y_step(3, 3)
    y_final(1)
    y_final(2)
    h_final()
    y_spread(0)
    for nh in range(2):
        d_step(nh, 2)
    y_final(3)
    y_spread(1)
    y_spread(2)
    for nh in range(2):
        d_step(nh, 3)
    load_m1.wait()
    load_m2.wait()
    y_spread(3)
    for nh in range(2):
        d_final(nh)
    adam()
    arrived(hgrad.at[other], hy_s, hy_r, pdev)
    for n in range(PARTS):
        y_end(n)
    for copy in sent:
        copy.wait_send()


def hand_over(yout, hgrad, *refs):
    weights, stream, heads, outs, sems = refs[:4], refs[4], refs[5], refs[6:10], refs[10]
    pairs = list(zip(weights, outs))
    for half in range(2):
        pairs.append((hgrad.at[half], heads.at[:, pl.ds(half * KHALF, KHALF)]))
    for n in range(PARTS):
        for q in range(4):
            pairs.append((yout.at[n, q], stream.at[pl.ds(q * QTOK, QTOK), pl.ds(n * WIDE, WIDE)]))
    copies = [pltpu.make_async_copy(src, dst, sems.at[i]) for i, (src, dst) in enumerate(pairs)]
    for copy in copies:
        copy.start()
    for copy in copies:
        copy.wait()


def shards(heads_out, residual, master, moment_one, moment_two, out_grad):
    any_spec = pl.BlockSpec(memory_space=pl.ANY)
    dma = pltpu.SemaphoreType.DMA
    vmem = pltpu.VMEM
    weights = pltpu.VMEM((ROWS, COLS), F32)
    outs = pl.pallas_call(
        kernel,
        out_shape=(
            vmem((PARTS, 4, QTOK, WIDE), BF16),
            vmem((2, QTOK, KHALF), BF16),
            weights, weights, weights, weights,
        ),
        in_specs=[any_spec] * 6,
        out_specs=[pl.BlockSpec(memory_space=vmem)] * 6,
        scratch_shapes=[
            vmem((8, QTOK, KHALF), BF16),
            vmem((2 * TOK, COLS), BF16),
            vmem((PARTS, 16, ROWS, WIDE), BF16),
            vmem((PARTS, 8, QTOK, WIDE), F32),
            vmem((PARTS, 2, 4, QTOK, WIDE), BF16),
            vmem((PARTS, 2, 4, QTOK, WIDE), BF16),
            vmem((QTOK, COLS), BF16),
            vmem((8, QTOK, KHALF), F32),
            vmem((2, 2, 2, QTOK, KHALF), BF16),
            vmem((2, 2, 2, QTOK, KHALF), BF16),
            vmem((2, QTOK, KHALF), BF16),
            vmem((16, ROWS, COLS), F32),
            vmem((8, ROWS, COLS), BF16),
            vmem((8, ROWS, COLS), BF16),
            vmem((2, 2, 4, ROWS, NHALF), BF16),
            vmem((2, 2, 4, ROWS, NHALF), BF16),
            vmem((ROWS, COLS), F32),
            vmem((ROWS, COLS), F32),
            vmem((ROWS, COLS), F32),
            dma((PARTS, 2, 4)), dma((PARTS, 2, 4)), dma((PARTS, 8)), dma((PARTS, 8)),
            dma((7,)), dma((7,)), dma((2,)), dma((2,)),
            dma((PARTS, 2, 4)), dma((PARTS, 2, 4)), dma((PARTS, 3)), dma((PARTS, 3)),
            dma((2, 2, 2)), dma((2, 2, 2)), dma, dma, dma, dma,
            dma((2, 2, 4)), dma((2, 2, 4)), dma((6,)),
        ],
        compiler_params=pltpu.CompilerParams(
            collective_id=0, has_side_effects=True, vmem_limit_bytes=40 << 20),
        cost_estimate=pl.CostEstimate(
            flops=6 * TOK * COLS * COLS, bytes_accessed=5 << 20, transcendentals=ROWS * COLS),
    )(*(pltpu.with_memory_space_constraint(v, pltpu.HBM)
        for v in (heads_out, residual, master, moment_one, moment_two, out_grad)))
    return tuple(pl.pallas_call(
        hand_over,
        out_shape=[pltpu.HBM((TOK, COLS), BF16), pltpu.HBM((QTOK, COLS), BF16)] + [pltpu.HBM((ROWS, COLS), F32)] * 4,
        in_specs=[any_spec] * 6,
        out_specs=[any_spec] * 6,
        scratch_shapes=[dma((6 + 4 * PARTS,))],
        compiler_params=pltpu.CompilerParams(vmem_limit_bytes=8 << 20),
    )(*outs))


def solution(mesh):
    return jax.shard_map(
        shards,
        mesh=mesh,
        in_specs=(
            P(("dp", "col"), "row"),
            P("dp", "col"),
            P(("row", "dp"), "col"),
            P(("row", "dp"), "col"),
            P(("row", "dp"), "col"),
            P("dp", "col"),
        ),
        out_specs=(
            P("dp", "col"),
            P(("dp", "col"), "row"),
            P(("row", "dp"), "col"),
            P(("row", "dp"), "col"),
            P(("row", "dp"), "col"),
            P(("row", "dp"), "col"),
        ),
        check_vma=False,
    )
```

```python
import math

import jax
import jax.numpy as jnp
from jax import lax
from jax.experimental import pallas as pl
from jax.experimental.pallas import tpu as pltpu
from jax.sharding import PartitionSpec as P

HEADS = 48
HEAD_DIM = 128

beta_one = 0.9
beta_two = 0.95
learn_rate = 0.1
weight_decay = 0.1
epsilon = 1e-08

MESH = pl.DeviceIdType.MESH
BF16, F32 = jnp.bfloat16, jnp.float32

NX, NY, NZ = 4, 8, 8
TOK = 256
QTOK = 64
KHALF = 768
COLS = 1536
NHALF = 768
PARTS = 4
WIDE = COLS // PARTS
ROWS = 48
SIDES = (1, -1)
SCALE = 1.0 / math.sqrt(HEADS * HEAD_DIM)


def reach(part, side, around):
    longer = around // 2
    return longer if part % 2 == side else around - 1 - longer


def kernel(
    h_ref, res_ref, master_ref, m1_ref, m2_ref, g_ref,
    yout, hgrad, wgv, nmv, n1v, n2v,
    hbuf, gbuf, wbuf, yp, ysend, yrecv, resv,
    hp, hsend, hrecv, hfin, dwp, dwx_send, dwx_recv, dsend, drecv,
    mv, m1v, m2v,
    wz_s, wz_r, wc_s, wc_r, hx_s, hx_r, gx_s, gx_r, y_s, y_r, ya_s, ya_r,
    dh_s, dh_r, hy_s, hy_r, dx_s, dx_r, dz_s, dz_r, loc,
):
    dp, yh, x = lax.axis_index("dp"), lax.axis_index("row"), lax.axis_index("col")
    c = lax.rem(dp, 2)
    z = lax.rem(lax.div(dp, 2), NZ)
    yl = lax.div(dp, 2 * NZ)
    y = 2 * yh + yl

    def wrap(v, n):
        return lax.rem(v + n, n)

    def device(dx=0, dy=0, dz=0, flip=False):
        yy = wrap(y + dy, NY)
        core = 1 - c if flip else c
        return ((lax.rem(yy, 2) * NZ + wrap(z + dz, NZ)) * 2 + core, lax.div(yy, 2), wrap(x + dx, NX))

    to_partner = 1 - 2 * yl
    zdev = [device(dz=s) for s in SIDES]
    xdev = [device(dx=s) for s in SIDES]
    ydev = [device(dy=s) for s in SIDES]
    y2dev = [device(dy=2 * s) for s in SIDES]
    cdev = device(flip=True)
    pdev = device(dy=to_partner)
    hidev = device(dy=-to_partner)

    sent = []

    def remote(src, dst, ssem, rsem, dev):
        return pltpu.make_async_remote_copy(
            src_ref=src, dst_ref=dst, send_sem=ssem, recv_sem=rsem, device_id=dev, device_id_type=MESH)

    def send(src, dst, ssem, rsem, dev):
        copy = remote(src, dst, ssem, rsem, dev)
        copy.start()
        sent.append(copy)

    def arrived(dst, ssem, rsem, dev):
        remote(dst, dst, ssem, rsem, dev).wait_recv()

    def own_cols(v):
        return pl.ds(pl.multiple_of(v * KHALF, KHALF), KHALF)

    load_master = pltpu.make_async_copy(master_ref, mv, loc.at[0])
    load_master.start()
    load_h = pltpu.make_async_copy(h_ref.at[:, own_cols(yl)], hbuf.at[yl * NX + x], loc.at[1])
    load_h.start()
    load_g = pltpu.make_async_copy(g_ref, gbuf.at[pl.ds(pl.multiple_of(yl * TOK, TOK), TOK)], loc.at[2])
    load_g.start()
    load_res = pltpu.make_async_copy(
        res_ref.at[pl.ds(pl.multiple_of(yh * QTOK, QTOK), QTOK)], resv, loc.at[3])
    load_res.start()
    load_m1 = pltpu.make_async_copy(m1_ref, m1v, loc.at[4])
    load_m1.start()
    load_m2 = pltpu.make_async_copy(m2_ref, m2v, loc.at[5])
    load_m2.start()

    def wz_send(n, side, s):
        slot = wbuf.at[n, wrap(z - SIDES[side] * s, NZ) * 2 + c]
        send(slot, slot, wz_s.at[n, side, s], wz_r.at[n, side, s], zdev[side])

    def wc_send(n, k, zz):
        slot = wbuf.at[n, zz * 2 + c]
        send(slot, slot, wc_s.at[n, k], wc_r.at[n, k], cdev)

    def wz_step(n, s):
        for side in range(2):
            if s <= reach(n, side, NZ):
                zz = wrap(z - SIDES[side] * s, NZ)
                arrived(wbuf.at[n, zz * 2 + c], wz_s.at[n, side, s - 1], wz_r.at[n, side, s - 1], zdev[side])
                if s < reach(n, side, NZ):
                    wz_send(n, side, s)
                wc_send(n, s if side == 0 else reach(n, 0, NZ) + s, zz)

    def wc_wait(n):
        for k in range(NZ):
            up = reach(n, 0, NZ)
            zz = z if k == 0 else wrap(z - k, NZ) if k <= up else wrap(z + (k - up), NZ)
            arrived(wbuf.at[n, zz * 2 + 1 - c], wc_s.at[n, k], wc_r.at[n, k], cdev)

    other = 1 - yl
    half = TOK // 2
    g_first = pl.ds(pl.multiple_of(other * half, half), half)
    g_there = pl.ds(pl.multiple_of(yl * TOK + other * half, half), half)
    g_last = pl.ds(pl.multiple_of(yl * half, half), half)
    g_goal = pl.ds(pl.multiple_of(yl * TOK + yl * half, half), half)

    def hx_send(src, slot, k, dev):
        send(src, hbuf.at[slot], hx_s.at[k], hx_r.at[k], dev)

    def h_arrived(slot, k):
        arrived(hbuf.at[slot], hx_s.at[k], hx_r.at[k], pdev)

    def h_far(g, k):
        step = 1 - 2 * g
        slot = g * NX + wrap(x - step, NX)
        hx_send(hbuf.at[slot], slot, k, device(dx=step))

    def y_slot(v):
        yy = wrap(v, NY)
        return lax.rem(yy, 2) * 4 + lax.div(yy, 2)

    def y_dot(n):
        h = hbuf[...].reshape(2 * TOK, KHALF)
        part = jnp.dot(h, wbuf[n].reshape(KHALF, WIDE), preferred_element_type=F32) * SCALE
        yp[n] = part.reshape(8, QTOK, WIDE)

    def y_step(n, s):
        for side in range(2):
            hops = reach(n, side, NY)
            if s < hops:
                value = yp[n, y_slot(y + SIDES[side] * (hops - s))]
                if s:
                    arrived(yrecv.at[n, side, s - 1], y_s.at[n, side, s - 1], y_r.at[n, side, s - 1], ydev[side])
                    value = value + yrecv[n, side, s - 1].astype(F32)
                ysend[n, side, s] = value.astype(BF16)
                send(ysend.at[n, side, s], yrecv.at[n, side, s], y_s.at[n, side, s], y_r.at[n, side, s], ydev[side])

    def y_final(n):
        value = yp[n, y_slot(y)] + resv[:, n * WIDE:(n + 1) * WIDE].astype(F32)
        for side in range(2):
            last = reach(n, side, NY) - 1
            arrived(yrecv.at[n, side, last], y_s.at[n, side, last], y_r.at[n, side, last], ydev[side])
            value = value + yrecv[n, side, last].astype(F32)
        yout[n, yh] = value.astype(BF16)
        for side in range(2):
            send(yout.at[n, yh], yout.at[n, yh], ya_s.at[n, side], ya_r.at[n, side], y2dev[side])

    def ya_arrived(n, k, q):
        arrived(yout.at[n, q], ya_s.at[n, k], ya_r.at[n, k], y2dev[0])

    def y_spread(n):
        order = (0, 1) if n % 2 == 0 else (1, 0)
        for side in order:
            q = wrap(yh - SIDES[side], 4)
            ya_arrived(n, side, q)
            if side == n % 2:
                send(yout.at[n, q], yout.at[n, q], ya_s.at[n, 2], ya_r.at[n, 2], y2dev[side])

    def y_end(n):
        q = wrap(yh + 2, 4)
        ya_arrived(n, 2, q)

    def h_dot():
        for t in range(2):
            rows = pl.ds(t * 256, 256)
            total = None
            for n in range(PARTS):
                w = wbuf[n].reshape(KHALF, WIDE)
                part = lax.dot_general(
                    gbuf[rows, n * WIDE:(n + 1) * WIDE], w, (((1,), (1,)), ((), ())),
                    preferred_element_type=F32)
                total = part if total is None else total + part
            hp[t * 4:(t + 1) * 4] = (total * SCALE).reshape(4, QTOK, KHALF)

    def h_step(s):
        for g in range(2):
            for side in range(2):
                hops = reach(g, side, NX)
                if s < hops:
                    value = hp[g * NX + wrap(x + SIDES[side] * (hops - s), NX)]
                    if s:
                        arrived(hrecv.at[g, side, s - 1], dh_s.at[g, side, s - 1], dh_r.at[g, side, s - 1], xdev[side])
                        value = value + hrecv[g, side, s - 1].astype(F32)
                    hsend[g, side, s] = value.astype(BF16)
                    send(hsend.at[g, side, s], hrecv.at[g, side, s], dh_s.at[g, side, s], dh_r.at[g, side, s], xdev[side])

    def h_final():
        for g in range(2):
            value = hp[g * NX + x]
            for side in range(2):
                last = reach(g, side, NX) - 1
                arrived(hrecv.at[g, side, last], dh_s.at[g, side, last], dh_r.at[g, side, last], xdev[side])
                value = value + hrecv[g, side, last].astype(F32)
            hfin[g] = value.astype(BF16)
        send(hfin.at[other], hgrad.at[yl], hy_s, hy_r, pdev)
        hgrad[yl] = hfin[yl]

    def d_dot():
        h = hbuf[...].reshape(2 * TOK, KHALF)
        for t in range(COLS // 256):
            part = lax.dot_general(
                h, gbuf[:, t * 256:(t + 1) * 256], (((0,), (0,)), ((), ())), preferred_element_type=F32)
            dwp[:, :, t * 256:(t + 1) * 256] = (part * SCALE).reshape(16, ROWS, 256)

    def d_cross():
        for zz in range(NZ):
            dwx_send[zz] = dwp[zz * 2 + 1 - c].astype(BF16)
            send(dwx_send.at[zz], dwx_recv.at[zz], dx_s.at[zz], dx_r.at[zz], cdev)

    def d_piece(nh, zz):
        cols = slice(nh * NHALF, (nh + 1) * NHALF)
        return dwp[zz * 2 + c, :, cols] + dwx_recv[zz, :, cols].astype(F32)

    def d_step(nh, s):
        for side in range(2):
            hops = reach(nh, side, NZ)
            if s < hops:
                value = d_piece(nh, wrap(z + SIDES[side] * (hops - s), NZ))
                if s:
                    arrived(drecv.at[nh, side, s - 1], dz_s.at[nh, side, s - 1], dz_r.at[nh, side, s - 1], zdev[side])
                    value = value + drecv[nh, side, s - 1].astype(F32)
                dsend[nh, side, s] = value.astype(BF16)
                send(dsend.at[nh, side, s], drecv.at[nh, side, s], dz_s.at[nh, side, s], dz_r.at[nh, side, s], zdev[side])

    def d_final(nh):
        value = d_piece(nh, z)
        for side in range(2):
            last = reach(nh, side, NZ) - 1
            arrived(drecv.at[nh, side, last], dz_s.at[nh, side, last], dz_r.at[nh, side, last], zdev[side])
            value = value + drecv[nh, side, last].astype(F32)
        wgv[:, nh * NHALF:(nh + 1) * NHALF] = value

    def adam():
        grad = wgv[...]
        master = mv[...]
        new_one = beta_one * m1v[...] + (1.0 - beta_one) * grad
        new_two = beta_two * m2v[...] + (1.0 - beta_two) * grad * grad
        bias_one = 1.0 - beta_one**10
        bias_two = 1.0 - beta_two**10
        direction = new_one / bias_one / (jnp.sqrt(new_two / bias_two) + epsilon)
        n1v[...] = new_one
        n2v[...] = new_two
        nmv[...] = master - learn_rate * (direction + weight_decay * master)

    barrier = pltpu.get_barrier_semaphore()
    around = zdev + xdev + ydev + y2dev + [cdev]
    for dev in around:
        pl.semaphore_signal(barrier, inc=1, device_id=dev, device_id_type=MESH)
    load_master.wait()
    own = z * 2 + c
    for n in range(PARTS):
        wbuf[n, own] = mv[:, n * WIDE:(n + 1) * WIDE].astype(BF16)
    pl.semaphore_wait(barrier, len(around))

    for side in range(2):
        wz_send(0, side, 0)
    hx_send(h_ref.at[:, own_cols(other)], yl * NX + x, 0, pdev)
    for side in range(2):
        hx_send(h_ref.at[:, own_cols(yl)], yl * NX + x, 1 + side, xdev[side])
    for side in range(2):
        wz_send(1, side, 0)
    for n in range(2, PARTS):
        for side in range(2):
            wz_send(n, side, 0)

    for n in range(PARTS):
        wc_send(n, 0, z)
    wz_step(0, 1)
    wz_step(1, 1)
    h_arrived(other * NX + x, 0)
    for side in range(2):
        hx_send(hbuf.at[other * NX + x], other * NX + x, 3 + side, xdev[side])
    send(g_ref.at[g_first], gbuf.at[g_there], gx_s.at[0], gx_r.at[0], hidev)
    wz_step(2, 1)
    wz_step(3, 1)
    for side in range(2):
        h_arrived(yl * NX + wrap(x - SIDES[side], NX), 1 + side)
    h_far(yl, 5)
    send(g_ref.at[g_last], gbuf.at[g_goal], gx_s.at[1], gx_r.at[1], pdev)
    wz_step(0, 2)
    wz_step(1, 2)
    wz_step(2, 2)
    for side in range(2):
        h_arrived(other * NX + wrap(x - SIDES[side], NX), 3 + side)
    h_far(other, 6)
    wz_step(3, 2)
    for n in range(PARTS):
        wz_step(n, 3)
    wz_step(0, 4)
    load_h.wait()
    h_arrived(yl * NX + wrap(x + 2, NX), 5)
    h_arrived(other * NX + wrap(x + 2, NX), 6)
    wc_wait(0)
    y_dot(0)
    y_step(0, 0)
    wz_step(1, 4)
    wz_step(2, 4)
    wz_step(3, 4)
    wc_wait(1)
    y_dot(1)
    y_step(1, 0)
    wc_wait(2)
    y_dot(2)
    y_step(2, 0)
    y_step(0, 1)
    wc_wait(3)
    y_dot(3)
    y_step(3, 0)
    load_g.wait()
    arrived(gbuf.at[g_there], gx_s.at[0], gx_r.at[0], hidev)
    arrived(gbuf.at[g_goal], gx_s.at[1], gx_r.at[1], pdev)
    y_step(1, 1)
    d_dot()
    d_cross()
    y_step(2, 1)
    y_step(0, 2)
    y_step(3, 1)
    y_step(1, 2)
    y_step(2, 2)
    for zz in range(NZ):
        arrived(dwx_recv.at[zz], dx_s.at[zz], dx_r.at[zz], cdev)
    for nh in range(2):
        d_step(nh, 0)
    h_dot()
    h_step(0)
    y_step(0, 3)
    y_step(3, 2)
    y_step(1, 3)
    y_step(2, 3)
    load_res.wait()
    y_final(0)
    for nh in range(2):
        d_step(nh, 1)
    y_step(3, 3)
    h_step(1)
    y_final(1)
    y_final(2)
    y_spread(0)
    for nh in range(2):
        d_step(nh, 2)
    y_final(3)
    h_final()
    y_spread(1)
    y_spread(2)
    for nh in range(2):
        d_step(nh, 3)
    load_m1.wait()
    load_m2.wait()
    y_spread(3)
    for nh in range(2):
        d_final(nh)
    adam()
    arrived(hgrad.at[other], hy_s, hy_r, pdev)
    for n in range(PARTS):
        y_end(n)
    for copy in sent:
        copy.wait_send()


def hand_over(yout, hgrad, *refs):
    weights, stream, heads, outs, sems = refs[:4], refs[4], refs[5], refs[6:10], refs[10]
    pairs = list(zip(weights, outs))
    for half in range(2):
        pairs.append((hgrad.at[half], heads.at[:, pl.ds(half * KHALF, KHALF)]))
    for n in range(PARTS):
        for q in range(4):
            pairs.append((yout.at[n, q], stream.at[pl.ds(q * QTOK, QTOK), pl.ds(n * WIDE, WIDE)]))
    copies = [pltpu.make_async_copy(src, dst, sems.at[i]) for i, (src, dst) in enumerate(pairs)]
    for copy in copies:
        copy.start()
    for copy in copies:
        copy.wait()


def shards(heads_out, residual, master, moment_one, moment_two, out_grad):
    any_spec = pl.BlockSpec(memory_space=pl.ANY)
    dma = pltpu.SemaphoreType.DMA
    vmem = pltpu.VMEM
    weights = pltpu.VMEM((ROWS, COLS), F32)
    outs = pl.pallas_call(
        kernel,
        out_shape=(
            vmem((PARTS, 4, QTOK, WIDE), BF16),
            vmem((2, QTOK, KHALF), BF16),
            weights, weights, weights, weights,
        ),
        in_specs=[any_spec] * 6,
        out_specs=[pl.BlockSpec(memory_space=vmem)] * 6,
        scratch_shapes=[
            vmem((8, QTOK, KHALF), BF16),
            vmem((2 * TOK, COLS), BF16),
            vmem((PARTS, 16, ROWS, WIDE), BF16),
            vmem((PARTS, 8, QTOK, WIDE), F32),
            vmem((PARTS, 2, 4, QTOK, WIDE), BF16),
            vmem((PARTS, 2, 4, QTOK, WIDE), BF16),
            vmem((QTOK, COLS), BF16),
            vmem((8, QTOK, KHALF), F32),
            vmem((2, 2, 2, QTOK, KHALF), BF16),
            vmem((2, 2, 2, QTOK, KHALF), BF16),
            vmem((2, QTOK, KHALF), BF16),
            vmem((16, ROWS, COLS), F32),
            vmem((8, ROWS, COLS), BF16),
            vmem((8, ROWS, COLS), BF16),
            vmem((2, 2, 4, ROWS, NHALF), BF16),
            vmem((2, 2, 4, ROWS, NHALF), BF16),
            vmem((ROWS, COLS), F32),
            vmem((ROWS, COLS), F32),
            vmem((ROWS, COLS), F32),
            dma((PARTS, 2, 4)), dma((PARTS, 2, 4)), dma((PARTS, 8)), dma((PARTS, 8)),
            dma((7,)), dma((7,)), dma((2,)), dma((2,)),
            dma((PARTS, 2, 4)), dma((PARTS, 2, 4)), dma((PARTS, 3)), dma((PARTS, 3)),
            dma((2, 2, 2)), dma((2, 2, 2)), dma, dma, dma((8,)), dma((8,)),
            dma((2, 2, 4)), dma((2, 2, 4)), dma((6,)),
        ],
        compiler_params=pltpu.CompilerParams(
            collective_id=0, has_side_effects=True, vmem_limit_bytes=40 << 20),
        cost_estimate=pl.CostEstimate(
            flops=6 * TOK * COLS * COLS, bytes_accessed=5 << 20, transcendentals=ROWS * COLS),
    )(*(pltpu.with_memory_space_constraint(v, pltpu.HBM)
        for v in (heads_out, residual, master, moment_one, moment_two, out_grad)))
    return tuple(pl.pallas_call(
        hand_over,
        out_shape=[pltpu.HBM((TOK, COLS), BF16), pltpu.HBM((QTOK, COLS), BF16)] + [pltpu.HBM((ROWS, COLS), F32)] * 4,
        in_specs=[any_spec] * 6,
        out_specs=[any_spec] * 6,
        scratch_shapes=[dma((6 + 4 * PARTS,))],
        compiler_params=pltpu.CompilerParams(vmem_limit_bytes=8 << 20),
    )(*outs))


def solution(mesh):
    return jax.shard_map(
        shards,
        mesh=mesh,
        in_specs=(
            P(("dp", "col"), "row"),
            P("dp", "col"),
            P(("row", "dp"), "col"),
            P(("row", "dp"), "col"),
            P(("row", "dp"), "col"),
            P("dp", "col"),
        ),
        out_specs=(
            P("dp", "col"),
            P(("dp", "col"), "row"),
            P(("row", "dp"), "col"),
            P(("row", "dp"), "col"),
            P(("row", "dp"), "col"),
            P(("row", "dp"), "col"),
        ),
        check_vma=False,
    )
```
